32 devices in a mesh: island: 4 (over y, x), fsdp: 8 (over z, core).
Axes of the slice: x: 2, y: 2, z: 4, core: 2. Of those that a mesh axis runs over, the one named last changes fastest.
Arguments:
- global_params: bfloat16 [4, 1, 4096, 8192], P('island', None, 'fsdp'), may hold values from -6 to 6
- local_params: bfloat16 [4, 1, 4096, 8192], P('island', None, 'fsdp'), may hold values from -6 to 6
- momentum: bfloat16 [4, 1, 4096, 8192], P('island', None, 'fsdp'), may hold values from -6 to 6
- init_factors: float32 [4, 1, 4, 8192], replicated, may hold values from -6 to 6
- seeds: int32 [4], replicated, may hold values from 0 to 3, as said below
- plan: int32 [8], replicated, may hold values from 1 to 2, as said below
- round_index: int32 [], replicated, may hold values from 0 to 999
Outputs:
- new_params: bfloat16 [4, 1, 4096, 8192], P('island', None, 'fsdp')
- new_momentum: bfloat16 [4, 1, 4096, 8192], P('island', None, 'fsdp')
- warm_factors: float32 [4, 1, 4, 8192], P('island')
The draws below stay inside these ranges and needn't reach their ends.
Inputs may be any that keep to these rules, and one draw needn't show every extreme that they name: `plan`: every entry is a power of two; every power of two up to 2 appears. `seeds`: every value from 0 to 3 is used by some replica.
All inputs are finite; a program needn't handle non-finite values.
Results may differ from the reference program's by a relative error of at most 0.0017.
Values sent between devices are 32-bit elements; how exact they have to be, the bound alone decides.
A program may use at most 128 MiB of HBM per device.

```python
import math
import jax
import jax.numpy as jnp
from jax import lax

COLS = 8192
ROWS = 4096
MATS = 1
RANK = 4
ITERS = 3
NSEED = 4
ROUNDS = 8
ISL = 4
N_ISLAND = 4


def draw_plan(key, part):
    levels = int(math.log2(N_ISLAND))
    covered = jax.random.permutation(jax.random.fold_in(key, 17), levels).astype(jnp.int32)
    others = jax.random.randint(jax.random.fold_in(key, 23), (ROUNDS - levels,), 0, levels).astype(jnp.int32)
    powers = jnp.concatenate([covered, others]).astype(jnp.int32)
    return jnp.left_shift(jnp.int32(1), powers).astype(jnp.int32)


def draw_seeds(key, part):
    order = jax.random.permutation(jax.random.fold_in(key, 29), ISL).astype(jnp.int32)
    return jnp.mod(order, NSEED).astype(jnp.int32)


def shard_levels(own_key, dims, shards, smallest, high):
    def one(position, blocks):
        heights = jax.random.uniform(jax.random.fold_in(jax.random.fold_in(own_key, 6), position), (blocks,), jnp.float32, smallest / len(shards), high / len(shards))
        return jnp.repeat(jnp.exp(heights), dims[position] // blocks).reshape((-1,) + (1,) * (len(dims) - position - 1))

    factor_of = one(*shards[0])
    for cut in shards[1:]:
        factor_of = factor_of * one(*cut)
    return factor_of


def centred(rng, dims, scale, reach, shards=(), held_as=jnp.bfloat16):
    drawn = scale * jax.random.normal(rng, dims, jnp.float32)
    if shards:
        drawn = drawn * shard_levels(rng, dims, shards, -0.22, 0.18)
    return jnp.clip(drawn, -reach, reach).astype(held_as)


def setup_inputs(seed: int = 0) -> dict:
    key_of = jax.random.split(jax.random.key(seed), 8)
    global_params = centred(key_of[0], (ISL, MATS, ROWS, COLS), 1.0, 6.0, ((0, 4), (2, 8)))
    local_params = centred(key_of[1], (ISL, MATS, ROWS, COLS), 1.0, 6.0, ((0, 4), (2, 8)))
    momentum = centred(key_of[2], (ISL, MATS, ROWS, COLS), 1.0, 6.0, ((0, 4), (2, 8)))
    init_factors = centred(key_of[3], (NSEED, MATS, RANK, COLS), 1.0, 6.0, (), jnp.float32)
    seeds = draw_seeds(jax.random.fold_in(key_of[7], 71), 0)
    plan = draw_plan(jax.random.fold_in(key_of[7], 71), 0)
    round_index = jax.random.randint(key_of[6], (), 0, 1000).astype(jnp.int32)
    return {"global_params": global_params, "local_params": local_params, "momentum": momentum, "init_factors": init_factors, "seeds": seeds, "plan": plan, "round_index": round_index}


def reference(global_params, local_params, momentum, init_factors, seeds, plan, round_index):
    high = lax.Precision.HIGHEST
    offset = plan[jnp.mod(round_index, plan.shape[0])]

    def one_replica(island_pos):
        partner = jnp.bitwise_xor(island_pos, offset).astype(jnp.int32)
        start = global_params[island_pos].astype(jnp.float32)
        delta = start - local_params[island_pos].astype(jnp.float32)
        other = global_params[partner].astype(jnp.float32) - local_params[partner].astype(jnp.float32)
        diff = delta - other
        factor = init_factors[seeds[jnp.minimum(island_pos, partner)]]
        basis = None
        for turn in range(ITERS):
            left = jnp.einsum('mkc,mrc->mkr', factor, diff, precision=high)
            gram = jnp.einsum('mkr,mjr->mkj', left, left, precision=high)
            lower = jnp.linalg.cholesky(gram)
            basis = lax.linalg.triangular_solve(lower, left, left_side=True, lower=True)
            factor = jnp.einsum('mkr,mrc->mkc', basis, diff, precision=high)
        correction = jnp.einsum('mkr,mkc->mrc', basis, factor, precision=high)
        gossiped = delta - 0.5 * correction
        velocity = 0.9 * momentum[island_pos].astype(jnp.float32) + gossiped
        updated = start - 0.7 * (gossiped + 0.9 * velocity)
        return (updated.astype(jnp.bfloat16), velocity.astype(jnp.bfloat16), factor)
    return lax.map(one_replica, jnp.arange(N_ISLAND, dtype=jnp.int32))
```

```python
import functools

import jax
import jax.numpy as jnp
from jax import lax
from jax.experimental import pallas as pl
from jax.experimental.pallas import tpu as pltpu
from jax.sharding import PartitionSpec as P

ITERS = 3
MESH = pl.DeviceIdType.MESH
F32, BF16 = jnp.float32, jnp.bfloat16
NT = (((1,), (1,)), ((), ()))
NN = (((1,), (0,)), ((), ()))


def dot(a, b, dims):
    return lax.dot_general(a, b, dims, preferred_element_type=F32)


def rounded(x):
    return x.astype(BF16).astype(F32)


def three_parts(x):
    high = rounded(x)
    rest = x - high
    middle = rounded(rest)
    return jnp.concatenate([high, middle, rest - middle, jnp.zeros_like(x)], axis=0).astype(BF16)


def folded(x, rank):
    return x[0:rank] + x[rank : 2 * rank] + x[2 * rank : 3 * rank]


def cholesky(gram, rank):
    lower, inverse = {}, {}
    for j in range(rank):
        square = gram[j : j + 1, j : j + 1]
        for k in range(j):
            square = square - lower[j, k] * lower[j, k]
        inverse[j] = 1.0 / jnp.sqrt(square)
        for i in range(j + 1, rank):
            entry = gram[i : i + 1, j : j + 1]
            for k in range(j):
                entry = entry - lower[i, k] * lower[j, k]
            lower[i, j] = entry * inverse[j]
    return lower, inverse


def solved(factors, x):
    lower, inverse = factors
    rows = []
    for i in range(x.shape[0]):
        row = x[i : i + 1]
        for k in range(i):
            row = row - lower[i, k] * rows[k]
        rows.append(row * inverse[i])
    return jnp.concatenate(rows, axis=0)


def gossip_kernel(
    level, shards, g_hbm, l_hbm, q_ref, warm_ref, fac_ref, bas_ref,
    hi, lo, g_buf, l_buf, qs, acc, p_out, p_in, rs_out, rs_in, gathered, grams,
    load_sem, p_sem, rs_send, rs_recv, ag_send, ag_recv, gram_send, gram_recv,
):
    rank, cols = q_ref.shape
    rows = hi.shape[0]
    members = 2 * shards
    width = cols // members
    island, shard = lax.axis_index("island"), lax.axis_index("fsdp")
    step = 1 << level
    side = lax.rem(lax.div(island, step), 2)
    me = side * shards + shard

    def device(k):
        return (island + (lax.div(k, shards) - side) * step, lax.rem(k, shards))

    def block(k):
        return pl.ds(pl.multiple_of(k * width, width), width)

    def after(k):
        return lax.rem(me + k, members)

    barrier = pltpu.get_barrier_semaphore()

    @pl.loop(1, members)
    def _(k):
        pl.semaphore_signal(barrier, inc=1, device_id=device(after(k)), device_id_type=MESH)

    part = g_buf.shape[1]
    parts = rows // part

    def load(i, slot):
        at = pl.ds(pl.multiple_of(i * part, part), part)
        return (
            pltpu.make_async_copy(g_hbm.at[at], g_buf.at[slot], load_sem.at[0, slot]),
            pltpu.make_async_copy(l_hbm.at[at], l_buf.at[slot], load_sem.at[1, slot]),
        )

    for copy in load(0, 0):
        copy.start()
    qs[...] = three_parts(q_ref[...])
    acc[...] = jnp.zeros_like(acc)
    piece = min(512, cols)

    @pl.loop(0, parts)
    def _(i):
        slot = lax.rem(i, 2)

        @pl.when(i + 1 < parts)
        def _():
            for copy in load(i + 1, 1 - slot):
                copy.start()

        for copy in load(i, slot):
            copy.wait()
        at = pl.ds(pl.multiple_of(i * part, part), part)
        total = jnp.zeros((part, 4 * rank), F32)
        for c in range(0, cols, piece):
            delta = g_buf[slot, :, c : c + piece].astype(F32) - l_buf[slot, :, c : c + piece].astype(F32)
            high = delta.astype(BF16)
            low = (delta - high.astype(F32)).astype(BF16)
            hi[at, c : c + piece] = high
            lo[at, c : c + piece] = low
            factor = qs[:, c : c + piece]
            total = total + dot(high, factor, NT) + dot(low, factor, NT)
        acc[at, 0 : 4 * rank] = total

    pl.semaphore_wait(barrier, members - 1)

    factors = None
    for turn in range(ITERS):
        product = folded(acc[...].T, rank)
        if turn:
            product = solved(factors, product)
        p_out[...] = product
        swap = pltpu.make_async_remote_copy(
            src_ref=p_out, dst_ref=p_in, send_sem=p_sem.at[0], recv_sem=p_sem.at[1],
            device_id=(island + (1 - 2 * side) * step, shard), device_id_type=MESH,
        )
        swap.start()
        swap.wait()
        left = product - p_in[...]

        lane = lax.broadcasted_iota(jnp.int32, (rank, 128), 1)
        gram = jnp.zeros((rank, 128), F32)
        for j in range(rank):
            column = jnp.sum(left * left[j : j + 1], axis=1, keepdims=True)
            gram = jnp.where(lane == j, column, gram)
        grams[turn, pl.ds(shard, 1)] = gram[None]

        def gram_copy(k):
            to = lax.rem(shard + k, shards)
            return pltpu.make_async_remote_copy(
                src_ref=grams.at[turn, shard], dst_ref=grams.at[turn, shard],
                send_sem=gram_send.at[turn, to], recv_sem=gram_recv.at[turn, shard],
                device_id=(island, to), device_id_type=MESH,
            )

        def gram_arrival(k):
            at = lax.rem(shard + k, shards)
            return pltpu.make_async_remote_copy(
                src_ref=grams.at[turn, at], dst_ref=grams.at[turn, at],
                send_sem=gram_send.at[turn, at], recv_sem=gram_recv.at[turn, at],
                device_id=(island, at), device_id_type=MESH,
            )

        @pl.loop(1, shards)
        def _(k):
            gram_copy(k).start()

        left_parts = three_parts(left)

        def raw(b):
            at = block(b)
            return folded(dot(left_parts, hi[:, at], NN) + dot(left_parts, lo[:, at], NN), rank)

        def scatter(b):
            return pltpu.make_async_remote_copy(
                src_ref=rs_out.at[b], dst_ref=rs_in.at[me],
                send_sem=rs_send.at[b], recv_sem=rs_recv.at[me],
                device_id=device(b), device_id_type=MESH,
            )

        def scatter_arrival(k):
            return pltpu.make_async_remote_copy(
                src_ref=rs_out.at[k], dst_ref=rs_in.at[k],
                send_sem=rs_send.at[k], recv_sem=rs_recv.at[k],
                device_id=device(k), device_id_type=MESH,
            )

        @pl.loop(1, members)
        def _(k):
            b = after(k)
            rs_out[pl.ds(b, 1)] = raw(b)[None]
            scatter(b).start()

        rs_in[pl.ds(me, 1)] = raw(me)[None]

        @pl.loop(1, members)
        def _(k):
            scatter_arrival(after(members - k)).wait_recv()

        gathered[pl.ds(me, 1)] = jnp.sum(rs_in[...], axis=0, keepdims=True)

        def gather(b):
            return pltpu.make_async_remote_copy(
                src_ref=gathered.at[me], dst_ref=gathered.at[me],
                send_sem=ag_send.at[b], recv_sem=ag_recv.at[me],
                device_id=device(b), device_id_type=MESH,
            )

        def gather_arrival(k):
            return pltpu.make_async_remote_copy(
                src_ref=gathered.at[k], dst_ref=gathered.at[k],
                send_sem=ag_send.at[k], recv_sem=ag_recv.at[k],
                device_id=device(k), device_id_type=MESH,
            )

        @pl.loop(1, members)
        def _(k):
            gather(after(k)).start()

        def normaliser():
            @pl.loop(1, shards)
            def _(k):
                gram_arrival(k).wait_recv()

            return cholesky(jnp.sum(grams[turn], axis=0), rank)

        if turn < ITERS - 1:

            def right(b):
                at = block(b)
                factor = three_parts(gathered[b])
                return dot(hi[:, at], factor, NT) + dot(lo[:, at], factor, NT)

            acc[:, 0 : 4 * rank] = right(me)

            @pl.loop(1, members)
            def _(k):
                b = after(members - k)
                gather_arrival(b).wait_recv()
                acc[:, 0 : 4 * rank] += right(b)

            factors = normaliser()
        else:
            factors = normaliser()
            basis = 0.5 * solved(factors, left)
            high = rounded(basis)
            stack = jnp.concatenate([high, high, basis - high, jnp.zeros_like(basis)], axis=0)
            bas_ref[...] = jnp.concatenate([stack, jnp.zeros((128 - 4 * rank, rows), F32)], axis=0).T.astype(BF16)

            def finish(b):
                at = block(b)
                factor = solved(factors, gathered[b])
                warm_ref[:, at] = factor
                high = rounded(factor)
                fac_ref[:, at] = jnp.concatenate([high, factor - high, high, jnp.zeros_like(high)], axis=0).astype(BF16)

            finish(me)

            @pl.loop(1, members)
            def _(k):
                b = after(members - k)
                gather_arrival(b).wait_recv()
                finish(b)

        @pl.loop(1, members)
        def _(k):
            b = after(k)
            scatter(b).wait_send()
            gather(b).wait_send()

        @pl.loop(1, shards)
        def _(k):
            gram_copy(k).wait_send()


def gossip(level, shards, g, l, q):
    rows, cols = g.shape
    rank = q.shape[0]
    members = 2 * shards
    width = cols // members
    part = min(64, rows)
    vmem = pl.BlockSpec(memory_space=pltpu.VMEM)
    hbm = pl.BlockSpec(memory_space=pl.ANY)
    dma = pltpu.SemaphoreType.DMA
    return pl.pallas_call(
        functools.partial(gossip_kernel, level, shards),
        out_shape=(
            jax.ShapeDtypeStruct((rank, cols), F32),
            jax.ShapeDtypeStruct((4 * rank, cols), BF16),
            jax.ShapeDtypeStruct((rows, 128), BF16),
        ),
        in_specs=[hbm, hbm, vmem],
        out_specs=(vmem, vmem, vmem),
        scratch_shapes=[
            pltpu.VMEM((rows, cols), BF16),
            pltpu.VMEM((rows, cols), BF16),
            pltpu.VMEM((2, part, cols), BF16),
            pltpu.VMEM((2, part, cols), BF16),
            pltpu.VMEM((4 * rank, cols), BF16),
            pltpu.VMEM((rows, 128), F32),
            pltpu.VMEM((rank, rows), F32),
            pltpu.VMEM((rank, rows), F32),
            pltpu.VMEM((members, rank, width), F32),
            pltpu.VMEM((members, rank, width), F32),
            pltpu.VMEM((members, rank, width), F32),
            pltpu.VMEM((ITERS, shards, rank, 128), F32),
            dma((2, 2)),
            dma((2,)),
            dma((members,)),
            dma((members,)),
            dma((members,)),
            dma((members,)),
            dma((ITERS, shards)),
            dma((ITERS, shards)),
        ],
        compiler_params=pltpu.CompilerParams(
            collective_id=level + 1, has_side_effects=True, vmem_limit_bytes=44 << 20
        ),
        cost_estimate=pl.CostEstimate(
            flops=12 * ITERS * rank * rows * cols, bytes_accessed=4 * rows * cols, transcendentals=0
        ),
    )(g, l, q)


def outer_kernel(bas_ref, fac_ref, g_ref, l_ref, m_ref, params_ref, momentum_ref):
    depth, cols = fac_ref.shape
    basis = bas_ref[:, 0:depth]
    piece = min(1024, cols)
    for c in range(0, cols, piece):
        at = slice(c, c + piece)
        start = g_ref[:, at].astype(F32)
        gossiped = start - l_ref[:, at].astype(F32) - dot(basis, fac_ref[:, at], NN)
        velocity = 0.9 * m_ref[:, at].astype(F32) + gossiped
        params_ref[:, at] = (start - 0.7 * (gossiped + 0.9 * velocity)).astype(BF16)
        momentum_ref[:, at] = velocity.astype(BF16)


def outer_step(bas, fac, g, l, m):
    rows, cols = g.shape
    part = min(32, rows)
    wide = pl.BlockSpec((part, cols), lambda i: (i, 0))
    return pl.pallas_call(
        outer_kernel,
        grid=(rows // part,),
        out_shape=(jax.ShapeDtypeStruct((rows, cols), BF16),) * 2,
        in_specs=[
            pl.BlockSpec((part, bas.shape[1]), lambda i: (i, 0)),
            pl.BlockSpec(fac.shape, lambda i: (0, 0)),
            wide, wide, wide,
        ],
        out_specs=(wide, wide),
        compiler_params=pltpu.CompilerParams(vmem_limit_bytes=24 << 20),
        cost_estimate=pl.CostEstimate(
            flops=2 * fac.shape[0] * rows * cols, bytes_accessed=10 * rows * cols, transcendentals=0
        ),
    )(bas, fac, g, l, m)


def on_device(global_params, local_params, momentum, init_factors, seeds, plan, round_index):
    shape = global_params.shape
    g, l, m = (x.reshape(shape[-2:]) for x in (global_params, local_params, momentum))
    offset = plan[jnp.mod(round_index, plan.shape[0])]
    island = lax.axis_index("island")
    factor = init_factors[seeds[jnp.minimum(island, jnp.bitwise_xor(island, offset))], 0]
    levels = lax.axis_size("island").bit_length() - 1
    shards = lax.axis_size("fsdp")
    level_ids = jnp.arange(levels, dtype=jnp.int32)
    which_bit = jnp.sum(jnp.where(jnp.left_shift(jnp.int32(1), level_ids) == offset, level_ids, 0))
    branches = [functools.partial(gossip, level, shards) for level in range(levels)]
    warm, fac, bas = lax.switch(which_bit, branches, g, l, factor)
    params, velocity = outer_step(bas, fac, g, l, m)
    return params.reshape(shape), velocity.reshape(shape), warm[None, None]


def solution(mesh):
    return jax.shard_map(
        on_device,
        mesh=mesh,
        in_specs=(
            P("island", None, "fsdp", None),
            P("island", None, "fsdp", None),
            P("island", None, "fsdp", None),
            P(),
            P(),
            P(),
            P(),
        ),
        out_specs=(
            P("island", None, "fsdp", None),
            P("island", None, "fsdp", None),
            P("island", None, None, None),
        ),
        check_vma=False,
    )
```

```python
import functools

import jax
import jax.numpy as jnp
from jax import lax
from jax.experimental import pallas as pl
from jax.experimental.pallas import tpu as pltpu
from jax.sharding import PartitionSpec as P

ITERS = 3
MESH = pl.DeviceIdType.MESH
F32, BF16 = jnp.float32, jnp.bfloat16
NT = (((1,), (1,)), ((), ()))
NN = (((1,), (0,)), ((), ()))


def dot(a, b, dims):
    return lax.dot_general(a, b, dims, preferred_element_type=F32)


def rounded(x):
    return x.astype(BF16).astype(F32)


def three_parts(x):
    high = rounded(x)
    rest = x - high
    middle = rounded(rest)
    return jnp.concatenate([high, middle, rest - middle, jnp.zeros_like(x)], axis=0).astype(BF16)


def folded(x, rank):
    return x[0:rank] + x[rank : 2 * rank] + x[2 * rank : 3 * rank]


def cholesky(gram, rank):
    lower, inverse = {}, {}
    for j in range(rank):
        square = gram[j : j + 1, j : j + 1]
        for k in range(j):
            square = square - lower[j, k] * lower[j, k]
        inverse[j] = 1.0 / jnp.sqrt(square)
        for i in range(j + 1, rank):
            entry = gram[i : i + 1, j : j + 1]
            for k in range(j):
                entry = entry - lower[i, k] * lower[j, k]
            lower[i, j] = entry * inverse[j]
    return lower, inverse


def solved(factors, x):
    lower, inverse = factors
    rows = []
    for i in range(x.shape[0]):
        row = x[i : i + 1]
        for k in range(i):
            row = row - lower[i, k] * rows[k]
        rows.append(row * inverse[i])
    return jnp.concatenate(rows, axis=0)


def gossip_kernel(
    level, shards, seeds_ref, g_hbm, l_hbm, init_ref, warm_ref, fac_ref, bas_ref,
    hi, lo, g_buf, l_buf, acc, p_out, p_in, rs_out, rs_in, gathered, grams,
    load_sem, p_sem, rs_send, rs_recv, ag_send, ag_recv, gram_send, gram_recv,
):
    rank, cols = init_ref.shape[1:]
    rows = hi.shape[0]
    members = 2 * shards
    width = cols // members
    bundle = 4 if members % 4 == 0 else 1
    bundles = members // bundle
    island, shard = lax.axis_index("island"), lax.axis_index("fsdp")
    step = 1 << level
    side = lax.rem(lax.div(island, step), 2)
    me = side * shards + shard

    def device(k):
        return (island + (lax.div(k, shards) - side) * step, lax.rem(k, shards))

    def block(k):
        return pl.ds(pl.multiple_of(k * width, width), width)

    def columns(k):
        return pl.ds(pl.multiple_of(k * (bundle * width), bundle * width), bundle * width)

    mine = lax.div(me, bundle)

    def others(k, act):
        for j in range(bundle):
            b = k * bundle + j

            @pl.when(b != me)
            def _():
                act(b)

    def after(k):
        return lax.rem(me + k, members)

    barrier = pltpu.get_barrier_semaphore()

    @pl.loop(1, members)
    def _(k):
        pl.semaphore_signal(barrier, inc=1, device_id=device(after(k)), device_id_type=MESH)

    part = g_buf.shape[2]
    parts = cols // part
    tall = min(32, rows)

    def load(i, slot):
        at = pl.ds(pl.multiple_of(i * part, part), part)
        return (
            pltpu.make_async_copy(g_hbm.at[:, at], g_buf.at[slot], load_sem.at[0, slot]),
            pltpu.make_async_copy(l_hbm.at[:, at], l_buf.at[slot], load_sem.at[1, slot]),
        )

    for copy in load(0, 0):
        copy.start()
    seed = seeds_ref[jnp.minimum(island, island + (1 - 2 * side) * step)]
    acc[...] = jnp.zeros_like(acc)

    def right(at, factor):
        parts = three_parts(factor)
        return dot(hi[:, at], parts, NT) + dot(lo[:, at], parts, NT)

    @pl.loop(0, parts)
    def _(i):
        slot = lax.rem(i, 2)

        @pl.when(i + 1 < parts)
        def _():
            for copy in load(i + 1, 1 - slot):
                copy.start()

        for copy in load(i, slot):
            copy.wait()
        at = pl.ds(pl.multiple_of(i * part, part), part)
        for r in range(0, rows, tall):
            delta = g_buf[slot, r : r + tall].astype(F32) - l_buf[slot, r : r + tall].astype(F32)
            high = delta.astype(BF16)
            hi[r : r + tall, at] = high
            lo[r : r + tall, at] = (delta - high.astype(F32)).astype(BF16)
        acc[:, 0 : 4 * rank] += right(at, init_ref[seed, :, at])

    pl.semaphore_wait(barrier, members - 1)

    factors = None
    for turn in range(ITERS):
        product = folded(acc[...].T, rank)
        if turn:
            product = solved(factors, product)
        p_out[...] = product
        swap = pltpu.make_async_remote_copy(
            src_ref=p_out, dst_ref=p_in, send_sem=p_sem.at[0], recv_sem=p_sem.at[1],
            device_id=(island + (1 - 2 * side) * step, shard), device_id_type=MESH,
        )
        swap.start()
        swap.wait()
        left = product - p_in[...]

        lane = lax.broadcasted_iota(jnp.int32, (rank, 128), 1)
        gram = jnp.zeros((rank, 128), F32)
        for j in range(rank):
            column = jnp.sum(left * left[j : j + 1], axis=1, keepdims=True)
            gram = jnp.where(lane == j, column, gram)
        grams[turn, pl.ds(shard, 1)] = gram[None]

        def gram_copy(k):
            to = lax.rem(shard + k, shards)
            return pltpu.make_async_remote_copy(
                src_ref=grams.at[turn, shard], dst_ref=grams.at[turn, shard],
                send_sem=gram_send.at[turn, to], recv_sem=gram_recv.at[turn, shard],
                device_id=(island, to), device_id_type=MESH,
            )

        def gram_arrival(k):
            at = lax.rem(shard + k, shards)
            return pltpu.make_async_remote_copy(
                src_ref=grams.at[turn, at], dst_ref=grams.at[turn, at],
                send_sem=gram_send.at[turn, at], recv_sem=gram_recv.at[turn, at],
                device_id=(island, at), device_id_type=MESH,
            )

        @pl.loop(1, shards)
        def _(k):
            gram_copy(k).start()

        left_parts = three_parts(left)

        def scatter(b):
            return pltpu.make_async_remote_copy(
                src_ref=rs_out.at[b], dst_ref=rs_in.at[me],
                send_sem=rs_send.at[b], recv_sem=rs_recv.at[me],
                device_id=device(b), device_id_type=MESH,
            )

        def scatter_arrival(k):
            return pltpu.make_async_remote_copy(
                src_ref=rs_out.at[k], dst_ref=rs_in.at[k],
                send_sem=rs_send.at[k], recv_sem=rs_recv.at[k],
                device_id=device(k), device_id_type=MESH,
            )

        @pl.loop(1, bundles + 1)
        def _(s):
            k = lax.rem(mine + s, bundles)
            at = columns(k)
            raw = folded(dot(left_parts, hi[:, at], NN) + dot(left_parts, lo[:, at], NN), rank)
            for j in range(bundle):
                rs_out[pl.ds(k * bundle + j, 1)] = raw[None, :, j * width : (j + 1) * width]
            others(k, lambda b: scatter(b).start())

        rs_in[pl.ds(me, 1)] = rs_out[pl.ds(me, 1)]

        @pl.loop(1, members)
        def _(k):
            scatter_arrival(after(members - k)).wait_recv()

        gathered[pl.ds(me, 1)] = jnp.sum(rs_in[...], axis=0, keepdims=True)

        def gather(b):
            return pltpu.make_async_remote_copy(
                src_ref=gathered.at[me], dst_ref=gathered.at[me],
                send_sem=ag_send.at[b], recv_sem=ag_recv.at[me],
                device_id=device(b), device_id_type=MESH,
            )

        def gather_arrival(k):
            return pltpu.make_async_remote_copy(
                src_ref=gathered.at[k], dst_ref=gathered.at[k],
                send_sem=ag_send.at[k], recv_sem=ag_recv.at[k],
                device_id=device(k), device_id_type=MESH,
            )

        @pl.loop(0, bundles)
        def _(s):
            others(lax.rem(mine + s, bundles), lambda b: gather(b).start())

        def normaliser():
            @pl.loop(1, shards)
            def _(k):
                gram_arrival(k).wait_recv()

            return cholesky(jnp.sum(grams[turn], axis=0), rank)

        if turn < ITERS - 1:

            @pl.loop(0, bundles)
            def _(s):
                k = lax.rem(mine + bundles - s, bundles)
                others(k, lambda b: gather_arrival(b).wait_recv())
                factor = jnp.concatenate([gathered[k * bundle + j] for j in range(bundle)], axis=1)
                total = right(columns(k), factor)

                @pl.when(s == 0)
                def _():
                    acc[:, 0 : 4 * rank] = total

                @pl.when(s > 0)
                def _():
                    acc[:, 0 : 4 * rank] += total

            factors = normaliser()
        else:
            factors = normaliser()
            basis = 0.5 * solved(factors, left)
            high = rounded(basis)
            stack = jnp.concatenate([high, high, basis - high, jnp.zeros_like(basis)], axis=0)
            bas_ref[...] = jnp.concatenate([stack, jnp.zeros((128 - 4 * rank, rows), F32)], axis=0).T.astype(BF16)

            def finish(b):
                at = block(b)
                factor = solved(factors, gathered[b])
                warm_ref[:, at] = factor
                high = rounded(factor)
                fac_ref[:, at] = jnp.concatenate([high, factor - high, high, jnp.zeros_like(high)], axis=0).astype(BF16)

            @pl.loop(0, bundles)
            def _(s):
                k = lax.rem(mine + bundles - s, bundles)
                others(k, lambda b: gather_arrival(b).wait_recv())
                for j in range(bundle):
                    finish(k * bundle + j)

        @pl.loop(1, members)
        def _(k):
            b = after(k)
            scatter(b).wait_send()
            gather(b).wait_send()

        @pl.loop(1, shards)
        def _(k):
            gram_copy(k).wait_send()


def gossip(level, shards, seeds, g, l, init):
    rows, cols = g.shape
    rank = init.shape[1]
    members = 2 * shards
    width = cols // members
    part = min(1024, cols)
    vmem = pl.BlockSpec(memory_space=pltpu.VMEM)
    hbm = pl.BlockSpec(memory_space=pl.ANY)
    dma = pltpu.SemaphoreType.DMA
    return pl.pallas_call(
        functools.partial(gossip_kernel, level, shards),
        out_shape=(
            jax.ShapeDtypeStruct((rank, cols), F32),
            jax.ShapeDtypeStruct((4 * rank, cols), BF16),
            jax.ShapeDtypeStruct((rows, 128), BF16),
        ),
        in_specs=[pl.BlockSpec(memory_space=pltpu.SMEM), hbm, hbm, vmem],
        out_specs=(vmem, vmem, vmem),
        scratch_shapes=[
            pltpu.VMEM((rows, cols), BF16),
            pltpu.VMEM((rows, cols), BF16),
            pltpu.VMEM((2, rows, part), BF16),
            pltpu.VMEM((2, rows, part), BF16),
            pltpu.VMEM((rows, 128), F32),
            pltpu.VMEM((rank, rows), F32),
            pltpu.VMEM((rank, rows), F32),
            pltpu.VMEM((members, rank, width), F32),
            pltpu.VMEM((members, rank, width), F32),
            pltpu.VMEM((members, rank, width), F32),
            pltpu.VMEM((ITERS, shards, rank, 128), F32),
            dma((2, 2)),
            dma((2,)),
            dma((members,)),
            dma((members,)),
            dma((members,)),
            dma((members,)),
            dma((ITERS, shards)),
            dma((ITERS, shards)),
        ],
        compiler_params=pltpu.CompilerParams(
            collective_id=level + 1, has_side_effects=True, vmem_limit_bytes=30 << 20
        ),
        cost_estimate=pl.CostEstimate(
            flops=12 * ITERS * rank * rows * cols, bytes_accessed=4 * rows * cols, transcendentals=0
        ),
    )(seeds, g, l, init)


def outer_kernel(bas_ref, fac_ref, g_ref, l_ref, m_ref, params_ref, momentum_ref, correction):
    depth = fac_ref.shape[0]
    rows = g_ref.shape[0]
    correction[...] = dot(bas_ref[:, 0:depth], fac_ref[...], NN)
    tall = min(32, rows)
    for r in range(0, rows, tall):
        at = slice(r, r + tall)
        start = g_ref[at].astype(F32)
        gossiped = start - l_ref[at].astype(F32) - correction[at]
        velocity = 0.9 * m_ref[at].astype(F32) + gossiped
        params_ref[at] = (start - 0.7 * (gossiped + 0.9 * velocity)).astype(BF16)
        momentum_ref[at] = velocity.astype(BF16)


def outer_step(bas, fac, g, l, m):
    rows, cols = g.shape
    part = min(512, cols)
    tile = pl.BlockSpec((rows, part), lambda i: (0, i))
    return pl.pallas_call(
        outer_kernel,
        grid=(cols // part,),
        out_shape=(jax.ShapeDtypeStruct((rows, cols), BF16),) * 2,
        in_specs=[
            pl.BlockSpec(bas.shape, lambda i: (0, 0)),
            pl.BlockSpec((fac.shape[0], part), lambda i: (0, i)),
            tile, tile, tile,
        ],
        out_specs=(tile, tile),
        scratch_shapes=[pltpu.VMEM((rows, part), F32)],
        compiler_params=pltpu.CompilerParams(vmem_limit_bytes=16 << 20),
        cost_estimate=pl.CostEstimate(
            flops=2 * fac.shape[0] * rows * cols, bytes_accessed=10 * rows * cols, transcendentals=0
        ),
    )(bas, fac, g, l, m)


def on_device(global_params, local_params, momentum, init_factors, seeds, plan, round_index):
    shape = global_params.shape
    g, l, m = (x.reshape(shape[-2:]) for x in (global_params, local_params, momentum))
    turns = jnp.arange(plan.shape[0], dtype=jnp.int32)
    offset = jnp.sum(jnp.where(turns == lax.rem(round_index, plan.shape[0]), plan, 0))
    levels = lax.axis_size("island").bit_length() - 1
    shards = lax.axis_size("fsdp")
    which_bit = sum((offset > 1 << level).astype(jnp.int32) for level in range(levels))
    branches = [functools.partial(gossip, level, shards) for level in range(levels)]
    warm, fac, bas = lax.switch(which_bit, branches, seeds, g, l, init_factors[:, 0])
    params, velocity = outer_step(bas, fac, g, l, m)
    return params.reshape(shape), velocity.reshape(shape), warm[None, None]


def solution(mesh):
    return jax.shard_map(
        on_device,
        mesh=mesh,
        in_specs=(
            P("island", None, "fsdp", None),
            P("island", None, "fsdp", None),
            P("island", None, "fsdp", None),
            P(),
            P(),
            P(),
            P(),
        ),
        out_specs=(
            P("island", None, "fsdp", None),
            P("island", None, "fsdp", None),
            P("island", None, None, None),
        ),
        check_vma=False,
    )
```

```python
import functools

import jax
import jax.numpy as jnp
from jax import lax
from jax.experimental import pallas as pl
from jax.experimental.pallas import tpu as pltpu
from jax.sharding import PartitionSpec as P

ITERS = 3
MESH = pl.DeviceIdType.MESH
F32, BF16 = jnp.float32, jnp.bfloat16
NT = (((1,), (1,)), ((), ()))
NN = (((1,), (0,)), ((), ()))


def dot(a, b, dims):
    return lax.dot_general(a, b, dims, preferred_element_type=F32)


def rounded(x):
    return x.astype(BF16).astype(F32)


def three_parts(x):
    high = rounded(x)
    rest = x - high
    middle = rounded(rest)
    return jnp.concatenate([high, middle, rest - middle, jnp.zeros_like(x)], axis=0).astype(BF16)


def folded(x, rank):
    return x[0:rank] + x[rank : 2 * rank] + x[2 * rank : 3 * rank]


def cholesky(gram, rank):
    lower, inverse = {}, {}
    for j in range(rank):
        square = gram[j : j + 1, j : j + 1]
        for k in range(j):
            square = square - lower[j, k] * lower[j, k]
        inverse[j] = 1.0 / jnp.sqrt(square)
        for i in range(j + 1, rank):
            entry = gram[i : i + 1, j : j + 1]
            for k in range(j):
                entry = entry - lower[i, k] * lower[j, k]
            lower[i, j] = entry * inverse[j]
    return lower, inverse


def solved(factors, x):
    lower, inverse = factors
    rows = []
    for i in range(x.shape[0]):
        row = x[i : i + 1]
        for k in range(i):
            row = row - lower[i, k] * rows[k]
        rows.append(row * inverse[i])
    return jnp.concatenate(rows, axis=0)


def gossip_kernel(
    level, shards, seeds_ref, g_hbm, l_hbm, init_ref, warm_ref, fac_ref, bas_ref,
    hi, lo, g_buf, l_buf, acc, p_out, p_in, rs_out, rs_in, gathered, grams,
    load_sem, p_sem, rs_send, rs_recv, ag_send, ag_recv, gram_send, gram_recv,
):
    rank, cols = init_ref.shape[1:]
    rows = hi.shape[0]
    members = 2 * shards
    width = cols // members
    bundle = 4 if members % 4 == 0 else 1
    bundles = members // bundle
    island, shard = lax.axis_index("island"), lax.axis_index("fsdp")
    step = 1 << level
    side = lax.rem(lax.div(island, step), 2)
    me = side * shards + shard

    def device(k):
        return (island + (lax.div(k, shards) - side) * step, lax.rem(k, shards))

    def block(k):
        return pl.ds(pl.multiple_of(k * width, width), width)

    def columns(k):
        return pl.ds(pl.multiple_of(k * (bundle * width), bundle * width), bundle * width)

    mine = lax.div(me, bundle)

    def others(k, act):
        for j in range(bundle):
            b = k * bundle + j

            @pl.when(b != me)
            def _():
                act(b)

    def after(k):
        return lax.rem(me + k, members)

    barrier = pltpu.get_barrier_semaphore()

    @pl.loop(1, members)
    def _(k):
        pl.semaphore_signal(barrier, inc=1, device_id=device(after(k)), device_id_type=MESH)

    part = g_buf.shape[2]
    parts = cols // part
    tall = min(64, rows)

    def load(i, slot):
        at = pl.ds(pl.multiple_of(i * part, part), part)
        return (
            pltpu.make_async_copy(g_hbm.at[:, at], g_buf.at[slot], load_sem.at[0, slot]),
            pltpu.make_async_copy(l_hbm.at[:, at], l_buf.at[slot], load_sem.at[1, slot]),
        )

    for copy in load(0, 0):
        copy.start()
    seed = seeds_ref[jnp.minimum(island, island + (1 - 2 * side) * step)]
    acc[...] = jnp.zeros_like(acc)

    def arrivals(ref, count, sem):
        pltpu.make_async_remote_copy(
            src_ref=ref.at[pl.ds(0, count)], dst_ref=ref.at[pl.ds(0, count)], send_sem=p_sem.at[0], recv_sem=sem,
            device_id=(island + (1 - 2 * side) * step, shard), device_id_type=MESH,
        ).wait_recv()

    def departures(ref, count, sem):
        pltpu.make_async_remote_copy(
            src_ref=ref.at[pl.ds(0, count)], dst_ref=ref.at[pl.ds(0, count)], send_sem=sem, recv_sem=p_sem.at[1],
            device_id=(island + (1 - 2 * side) * step, shard), device_id_type=MESH,
        ).wait_send()

    def right(at, factor):
        parts = three_parts(factor)
        return dot(hi[:, at], parts, NT) + dot(lo[:, at], parts, NT)

    @pl.loop(0, parts)
    def _(i):
        slot = lax.rem(i, 2)

        @pl.when(i + 1 < parts)
        def _():
            for copy in load(i + 1, 1 - slot):
                copy.start()

        for copy in load(i, slot):
            copy.wait()
        at = pl.ds(pl.multiple_of(i * part, part), part)
        factor = three_parts(init_ref[seed, :, at])
        for r in range(0, rows, tall):
            delta = g_buf[slot, r : r + tall].astype(F32) - l_buf[slot, r : r + tall].astype(F32)
            high = delta.astype(BF16)
            low = (delta - high.astype(F32)).astype(BF16)
            hi[r : r + tall, at] = high
            lo[r : r + tall, at] = low
            acc[r : r + tall, 0 : 4 * rank] += dot(high, factor, NT) + dot(low, factor, NT)

    pl.semaphore_wait(barrier, members - 1)

    factors = None
    for turn in range(ITERS):
        product = folded(acc[...].T, rank)
        if turn:
            product = solved(factors, product)
        p_out[...] = product
        swap = pltpu.make_async_remote_copy(
            src_ref=p_out, dst_ref=p_in, send_sem=p_sem.at[0], recv_sem=p_sem.at[1],
            device_id=(island + (1 - 2 * side) * step, shard), device_id_type=MESH,
        )
        swap.start()
        swap.wait()
        left = product - p_in[...]

        lane = lax.broadcasted_iota(jnp.int32, (rank, 128), 1)
        gram = jnp.zeros((rank, 128), F32)
        for j in range(rank):
            column = jnp.sum(left * left[j : j + 1], axis=1, keepdims=True)
            gram = jnp.where(lane == j, column, gram)
        grams[turn, pl.ds(shard, 1)] = gram[None]

        def gram_copy(k):
            to = lax.rem(shard + k, shards)
            return pltpu.make_async_remote_copy(
                src_ref=grams.at[turn, shard], dst_ref=grams.at[turn, shard],
                send_sem=gram_send, recv_sem=gram_recv.at[turn],
                device_id=(island, to), device_id_type=MESH,
            )

        @pl.loop(1, shards)
        def _(k):
            gram_copy(k).start()

        left_parts = three_parts(left)

        def scatter(b):
            return pltpu.make_async_remote_copy(
                src_ref=rs_out.at[b], dst_ref=rs_in.at[me],
                send_sem=rs_send, recv_sem=rs_recv,
                device_id=device(b), device_id_type=MESH,
            )

        @pl.loop(1, bundles + 1)
        def _(s):
            k = lax.rem(mine + s, bundles)
            at = columns(k)
            raw = folded(dot(left_parts, hi[:, at], NN) + dot(left_parts, lo[:, at], NN), rank)
            for j in range(bundle):
                rs_out[pl.ds(k * bundle + j, 1)] = raw[None, :, j * width : (j + 1) * width]
            others(k, lambda b: scatter(b).start())

        rs_in[pl.ds(me, 1)] = rs_out[pl.ds(me, 1)]

        arrivals(rs_in, members - 1, rs_recv)
        gathered[pl.ds(me, 1)] = jnp.sum(rs_in[...], axis=0, keepdims=True)

        def gather(b):
            return pltpu.make_async_remote_copy(
                src_ref=gathered.at[me], dst_ref=gathered.at[me],
                send_sem=ag_send, recv_sem=ag_recv.at[mine],
                device_id=device(b), device_id_type=MESH,
            )

        def gathered_bundle(s):
            k = lax.rem(mine + bundles - s, bundles)

            @pl.when(s > 0)
            def _():
                arrivals(gathered, bundle, ag_recv.at[k])

            if bundle > 1:

                @pl.when(s == 0)
                def _():
                    arrivals(gathered, bundle - 1, ag_recv.at[k])

            return k

        @pl.loop(0, bundles)
        def _(s):
            others(lax.rem(mine + s, bundles), lambda b: gather(b).start())

        def normaliser():
            arrivals(grams.at[turn], shards - 1, gram_recv.at[turn])
            return cholesky(jnp.sum(grams[turn], axis=0), rank)

        if turn < ITERS - 1:

            @pl.loop(0, bundles)
            def _(s):
                k = gathered_bundle(s)
                factor = jnp.concatenate([gathered[k * bundle + j] for j in range(bundle)], axis=1)
                total = right(columns(k), factor)

                @pl.when(s == 0)
                def _():
                    acc[:, 0 : 4 * rank] = total

                @pl.when(s > 0)
                def _():
                    acc[:, 0 : 4 * rank] += total

            factors = normaliser()
        else:
            factors = normaliser()
            basis = 0.5 * solved(factors, left)
            high = rounded(basis)
            stack = jnp.concatenate([high, high, basis - high, jnp.zeros_like(basis)], axis=0)
            bas_ref[...] = jnp.concatenate([stack, jnp.zeros((128 - 4 * rank, rows), F32)], axis=0).T.astype(BF16)

            def finish(b):
                at = block(b)
                factor = solved(factors, gathered[b])
                warm_ref[:, at] = factor
                high = rounded(factor)
                fac_ref[:, at] = jnp.concatenate([high, factor - high, high, jnp.zeros_like(high)], axis=0).astype(BF16)

            @pl.loop(0, bundles)
            def _(s):
                k = gathered_bundle(s)
                for j in range(bundle):
                    finish(k * bundle + j)

        departures(rs_out, members - 1, rs_send)
        departures(gathered, members - 1, ag_send)
        departures(grams.at[turn], shards - 1, gram_send)


def gossip(level, shards, seeds, g, l, init):
    rows, cols = g.shape
    rank = init.shape[1]
    members = 2 * shards
    width = cols // members
    bundles = members // 4 if members % 4 == 0 else members
    part = min(1024, cols)
    vmem = pl.BlockSpec(memory_space=pltpu.VMEM)
    hbm = pl.BlockSpec(memory_space=pl.ANY)
    dma = pltpu.SemaphoreType.DMA
    return pl.pallas_call(
        functools.partial(gossip_kernel, level, shards),
        out_shape=(
            jax.ShapeDtypeStruct((rank, cols), F32),
            jax.ShapeDtypeStruct((4 * rank, cols), BF16),
            jax.ShapeDtypeStruct((rows, 128), BF16),
        ),
        in_specs=[pl.BlockSpec(memory_space=pltpu.SMEM), hbm, hbm, vmem],
        out_specs=(vmem, vmem, vmem),
        scratch_shapes=[
            pltpu.VMEM((rows, cols), BF16),
            pltpu.VMEM((rows, cols), BF16),
            pltpu.VMEM((2, rows, part), BF16),
            pltpu.VMEM((2, rows, part), BF16),
            pltpu.VMEM((rows, 128), F32),
            pltpu.VMEM((rank, rows), F32),
            pltpu.VMEM((rank, rows), F32),
            pltpu.VMEM((members, rank, width), F32),
            pltpu.VMEM((members, rank, width), F32),
            pltpu.VMEM((members, rank, width), F32),
            pltpu.VMEM((ITERS, shards, rank, 128), F32),
            dma((2, 2)),
            dma((2,)),
            dma,
            dma,
            dma,
            dma((bundles,)),
            dma,
            dma((ITERS,)),
        ],
        compiler_params=pltpu.CompilerParams(
            collective_id=level + 1, has_side_effects=True, vmem_limit_bytes=30 << 20
        ),
        cost_estimate=pl.CostEstimate(
            flops=12 * ITERS * rank * rows * cols, bytes_accessed=4 * rows * cols, transcendentals=0
        ),
    )(seeds, g, l, init)


def outer_kernel(bas_ref, fac_ref, g_ref, l_ref, m_ref, params_ref, momentum_ref, correction):
    depth = fac_ref.shape[0]
    rows = g_ref.shape[0]
    correction[...] = dot(bas_ref[:, 0:depth], fac_ref[...], NN)
    tall = min(32, rows)
    for r in range(0, rows, tall):
        at = slice(r, r + tall)
        start = g_ref[at].astype(F32)
        gossiped = start - l_ref[at].astype(F32) - correction[at]
        velocity = 0.9 * m_ref[at].astype(F32) + gossiped
        params_ref[at] = (start - 0.7 * (gossiped + 0.9 * velocity)).astype(BF16)
        momentum_ref[at] = velocity.astype(BF16)


def outer_step(bas, fac, g, l, m):
    rows, cols = g.shape
    part = min(1024, cols)
    tile = pl.BlockSpec((rows, part), lambda i: (0, i))
    return pl.pallas_call(
        outer_kernel,
        grid=(cols // part,),
        out_shape=(jax.ShapeDtypeStruct((rows, cols), BF16),) * 2,
        in_specs=[
            pl.BlockSpec(bas.shape, lambda i: (0, 0)),
            pl.BlockSpec((fac.shape[0], part), lambda i: (0, i)),
            tile, tile, tile,
        ],
        out_specs=(tile, tile),
        scratch_shapes=[pltpu.VMEM((rows, part), F32)],
        compiler_params=pltpu.CompilerParams(vmem_limit_bytes=56 << 20),
        cost_estimate=pl.CostEstimate(
            flops=2 * fac.shape[0] * rows * cols, bytes_accessed=10 * rows * cols, transcendentals=0
        ),
    )(bas, fac, g, l, m)


def on_device(global_params, local_params, momentum, init_factors, seeds, plan, round_index):
    shape = global_params.shape
    g, l, m = (x.reshape(shape[-2:]) for x in (global_params, local_params, momentum))
    turns = jnp.arange(plan.shape[0], dtype=jnp.int32)
    offset = jnp.sum(jnp.where(turns == lax.rem(round_index, plan.shape[0]), plan, 0))
    levels = lax.axis_size("island").bit_length() - 1
    shards = lax.axis_size("fsdp")
    which_bit = sum((offset > 1 << level).astype(jnp.int32) for level in range(levels))
    branches = [functools.partial(gossip, level, shards) for level in range(levels)]
    warm, fac, bas = lax.switch(which_bit, branches, seeds, g, l, init_factors[:, 0])
    params, velocity = outer_step(bas, fac, g, l, m)
    return params.reshape(shape), velocity.reshape(shape), warm[None, None]


def solution(mesh):
    return jax.shard_map(
        on_device,
        mesh=mesh,
        in_specs=(
            P("island", None, "fsdp", None),
            P("island", None, "fsdp", None),
            P("island", None, "fsdp", None),
            P(),
            P(),
            P(),
            P(),
        ),
        out_specs=(
            P("island", None, "fsdp", None),
            P("island", None, "fsdp", None),
            P("island", None, None, None),
        ),
        check_vma=False,
    )
```

```python
import functools

import jax
import jax.numpy as jnp
from jax import lax
from jax.experimental import pallas as pl
from jax.experimental.pallas import tpu as pltpu
from jax.sharding import PartitionSpec as P

ITERS = 3
MESH = pl.DeviceIdType.MESH
F32, BF16 = jnp.float32, jnp.bfloat16
NT = (((1,), (1,)), ((), ()))
NN = (((1,), (0,)), ((), ()))


def dot(a, b, dims):
    return lax.dot_general(a, b, dims, preferred_element_type=F32)


def rounded(x):
    return x.astype(BF16).astype(F32)


def three_parts(x):
    high = rounded(x)
    rest = x - high
    middle = rounded(rest)
    return jnp.concatenate([high, middle, rest - middle, jnp.zeros_like(x)], axis=0).astype(BF16)


def folded(x, rank):
    return x[0:rank] + x[rank : 2 * rank] + x[2 * rank : 3 * rank]


def cholesky(gram, rank):
    lower, inverse = {}, {}
    for j in range(rank):
        square = gram[j : j + 1, j : j + 1]
        for k in range(j):
            square = square - lower[j, k] * lower[j, k]
        inverse[j] = 1.0 / jnp.sqrt(square)
        for i in range(j + 1, rank):
            entry = gram[i : i + 1, j : j + 1]
            for k in range(j):
                entry = entry - lower[i, k] * lower[j, k]
            lower[i, j] = entry * inverse[j]
    return lower, inverse


def solved(factors, x):
    lower, inverse = factors
    rows = []
    for i in range(x.shape[0]):
        row = x[i : i + 1]
        for k in range(i):
            row = row - lower[i, k] * rows[k]
        rows.append(row * inverse[i])
    return jnp.concatenate(rows, axis=0)


def gossip_kernel(
    level, shards, seeds_ref, g_hbm, l_hbm, m_hbm, init_ref, warm_ref, fac_ref, bas_ref, hi, lo, g_ref, m_ref,
    l_buf, acc, p_out, p_in, rs_out, rs_in, gathered, grams,
    load_sem, m_sem, p_sem, rs_send, rs_recv, ag_send, ag_recv, gram_send, gram_recv,
):
    rank, cols = init_ref.shape[1:]
    rows = hi.shape[0]
    members = 2 * shards
    width = cols // members
    bundle = 4 if members % 4 == 0 else 1
    bundles = members // bundle
    island, shard = lax.axis_index("island"), lax.axis_index("fsdp")
    step = 1 << level
    side = lax.rem(lax.div(island, step), 2)
    me = side * shards + shard

    def device(k):
        return (island + (lax.div(k, shards) - side) * step, lax.rem(k, shards))

    def block(k):
        return pl.ds(pl.multiple_of(k * width, width), width)

    def columns(k):
        return pl.ds(pl.multiple_of(k * (bundle * width), bundle * width), bundle * width)

    mine = lax.div(me, bundle)

    def others(k, act):
        for j in range(bundle):
            b = k * bundle + j

            @pl.when(b != me)
            def _():
                act(b)

    def after(k):
        return lax.rem(me + k, members)

    barrier = pltpu.get_barrier_semaphore()

    @pl.loop(1, members)
    def _(k):
        pl.semaphore_signal(barrier, inc=1, device_id=device(after(k)), device_id_type=MESH)

    part = l_buf.shape[2]
    parts = cols // part
    tall = min(64, rows)

    def load(i, slot):
        at = pl.ds(pl.multiple_of(i * part, part), part)
        return (
            pltpu.make_async_copy(g_hbm.at[:, at], g_ref.at[:, at], load_sem.at[0, slot]),
            pltpu.make_async_copy(l_hbm.at[:, at], l_buf.at[slot], load_sem.at[1, slot]),
        )

    for copy in load(0, 0):
        copy.start()
    seed = seeds_ref[jnp.minimum(island, island + (1 - 2 * side) * step)]
    acc[...] = jnp.zeros_like(acc)

    def arrivals(ref, count, sem):
        pltpu.make_async_remote_copy(
            src_ref=ref.at[pl.ds(0, count)], dst_ref=ref.at[pl.ds(0, count)], send_sem=p_sem.at[0], recv_sem=sem,
            device_id=(island + (1 - 2 * side) * step, shard), device_id_type=MESH,
        ).wait_recv()

    def departures(ref, count, sem):
        pltpu.make_async_remote_copy(
            src_ref=ref.at[pl.ds(0, count)], dst_ref=ref.at[pl.ds(0, count)], send_sem=sem, recv_sem=p_sem.at[1],
            device_id=(island + (1 - 2 * side) * step, shard), device_id_type=MESH,
        ).wait_send()

    def right(at, factor):
        parts = three_parts(factor)
        return dot(hi[:, at], parts, NT) + dot(lo[:, at], parts, NT)

    @pl.loop(0, parts)
    def _(i):
        slot = lax.rem(i, 2)

        @pl.when(i + 1 < parts)
        def _():
            for copy in load(i + 1, 1 - slot):
                copy.start()

        for copy in load(i, slot):
            copy.wait()
        at = pl.ds(pl.multiple_of(i * part, part), part)
        factor = three_parts(init_ref[seed, :, at])
        for r in range(0, rows, tall):
            delta = g_ref[r : r + tall, at].astype(F32) - l_buf[slot, r : r + tall].astype(F32)
            high = delta.astype(BF16)
            low = (delta - high.astype(F32)).astype(BF16)
            hi[r : r + tall, at] = high
            lo[r : r + tall, at] = low
            acc[r : r + tall, 0 : 4 * rank] += dot(high, factor, NT) + dot(low, factor, NT)

    fill = pltpu.make_async_copy(m_hbm, m_ref, m_sem)
    fill.start()
    pl.semaphore_wait(barrier, members - 1)

    factors = None
    for turn in range(ITERS):
        product = folded(acc[...].T, rank)
        if turn:
            product = solved(factors, product)
        p_out[...] = product
        swap = pltpu.make_async_remote_copy(
            src_ref=p_out, dst_ref=p_in, send_sem=p_sem.at[0], recv_sem=p_sem.at[1],
            device_id=(island + (1 - 2 * side) * step, shard), device_id_type=MESH,
        )
        swap.start()
        swap.wait()
        left = product - p_in[...]

        lane = lax.broadcasted_iota(jnp.int32, (rank, 128), 1)
        gram = jnp.zeros((rank, 128), F32)
        for j in range(rank):
            column = jnp.sum(left * left[j : j + 1], axis=1, keepdims=True)
            gram = jnp.where(lane == j, column, gram)
        grams[turn, pl.ds(shard, 1)] = gram[None]

        def gram_copy(k):
            to = lax.rem(shard + k, shards)
            return pltpu.make_async_remote_copy(
                src_ref=grams.at[turn, shard], dst_ref=grams.at[turn, shard],
                send_sem=gram_send, recv_sem=gram_recv.at[turn],
                device_id=(island, to), device_id_type=MESH,
            )

        @pl.loop(1, shards)
        def _(k):
            gram_copy(k).start()

        left_parts = three_parts(left)

        def scatter(b):
            return pltpu.make_async_remote_copy(
                src_ref=rs_out.at[b], dst_ref=rs_in.at[me],
                send_sem=rs_send, recv_sem=rs_recv,
                device_id=device(b), device_id_type=MESH,
            )

        @pl.loop(1, bundles + 1)
        def _(s):
            k = lax.rem(mine + s, bundles)
            at = columns(k)
            raw = folded(dot(left_parts, hi[:, at], NN) + dot(left_parts, lo[:, at], NN), rank)
            for j in range(bundle):
                rs_out[pl.ds(k * bundle + j, 1)] = raw[None, :, j * width : (j + 1) * width]
            others(k, lambda b: scatter(b).start())

        rs_in[pl.ds(me, 1)] = rs_out[pl.ds(me, 1)]

        arrivals(rs_in, members - 1, rs_recv)
        gathered[pl.ds(me, 1)] = jnp.sum(rs_in[...], axis=0, keepdims=True)

        def gather(b):
            return pltpu.make_async_remote_copy(
                src_ref=gathered.at[me], dst_ref=gathered.at[me],
                send_sem=ag_send, recv_sem=ag_recv.at[mine],
                device_id=device(b), device_id_type=MESH,
            )

        def gathered_bundle(s):
            k = lax.rem(mine + bundles - s, bundles)

            @pl.when(s > 0)
            def _():
                arrivals(gathered, bundle, ag_recv.at[k])

            if bundle > 1:

                @pl.when(s == 0)
                def _():
                    arrivals(gathered, bundle - 1, ag_recv.at[k])

            return k

        @pl.loop(0, bundles)
        def _(s):
            others(lax.rem(mine + s, bundles), lambda b: gather(b).start())

        def normaliser():
            arrivals(grams.at[turn], shards - 1, gram_recv.at[turn])
            return cholesky(jnp.sum(grams[turn], axis=0), rank)

        if turn < ITERS - 1:

            @pl.loop(0, bundles)
            def _(s):
                k = gathered_bundle(s)
                factor = jnp.concatenate([gathered[k * bundle + j] for j in range(bundle)], axis=1)
                total = right(columns(k), factor)

                @pl.when(s == 0)
                def _():
                    acc[:, 0 : 4 * rank] = total

                @pl.when(s > 0)
                def _():
                    acc[:, 0 : 4 * rank] += total

            factors = normaliser()
        else:
            factors = normaliser()
            basis = 0.5 * solved(factors, left)
            high = rounded(basis)
            stack = jnp.concatenate([high, high, basis - high, jnp.zeros_like(basis)], axis=0)
            bas_ref[...] = jnp.concatenate([stack, jnp.zeros((128 - 4 * rank, rows), F32)], axis=0).T.astype(BF16)

            def finish(b):
                at = block(b)
                factor = solved(factors, gathered[b])
                warm_ref[:, at] = factor
                high = rounded(factor)
                fac_ref[:, at] = jnp.concatenate([high, factor - high, high, jnp.zeros_like(high)], axis=0).astype(BF16)

            @pl.loop(0, bundles)
            def _(s):
                k = gathered_bundle(s)
                for j in range(bundle):
                    finish(k * bundle + j)

        departures(rs_out, members - 1, rs_send)
        departures(gathered, members - 1, ag_send)
        departures(grams.at[turn], shards - 1, gram_send)

    fill.wait()


def gossip(level, shards, seeds, g, l, m, init):
    rows, cols = g.shape
    rank = init.shape[1]
    members = 2 * shards
    width = cols // members
    bundles = members // 4 if members % 4 == 0 else members
    part = min(1024, cols)
    vmem = pl.BlockSpec(memory_space=pltpu.VMEM)
    hbm = pl.BlockSpec(memory_space=pl.ANY)
    dma = pltpu.SemaphoreType.DMA
    return pl.pallas_call(
        functools.partial(gossip_kernel, level, shards),
        out_shape=(
            jax.ShapeDtypeStruct((rank, cols), F32),
            jax.ShapeDtypeStruct((4 * rank, cols), BF16),
            jax.ShapeDtypeStruct((rows, 128), BF16),
        )
        + (pltpu.VMEM((rows, cols), BF16),) * 4,
        in_specs=[pl.BlockSpec(memory_space=pltpu.SMEM), hbm, hbm, hbm, vmem],
        out_specs=(vmem,) * 7,
        scratch_shapes=[
            pltpu.VMEM((2, rows, part), BF16),
            pltpu.VMEM((rows, 128), F32),
            pltpu.VMEM((rank, rows), F32),
            pltpu.VMEM((rank, rows), F32),
            pltpu.VMEM((members, rank, width), F32),
            pltpu.VMEM((members, rank, width), F32),
            pltpu.VMEM((members, rank, width), F32),
            pltpu.VMEM((ITERS, shards, rank, 128), F32),
            dma((2, 2)),
            dma,
            dma((2,)),
            dma,
            dma,
            dma,
            dma((bundles,)),
            dma,
            dma((ITERS,)),
        ],
        compiler_params=pltpu.CompilerParams(
            collective_id=level + 1, has_side_effects=True, vmem_limit_bytes=12 << 20
        ),
        cost_estimate=pl.CostEstimate(
            flops=12 * ITERS * rank * rows * cols, bytes_accessed=4 * rows * cols, transcendentals=0
        ),
    )(seeds, g, l, m, init)


def outer_kernel(bas_ref, fac_ref, hi, lo, g_ref, m_ref, params_ref, momentum_ref, correction):
    depth = fac_ref.shape[0]
    rows, part = params_ref.shape
    correction[...] = dot(bas_ref[:, 0:depth], fac_ref[...], NN)
    tall = min(32, rows)
    columns = pl.ds(pl.multiple_of(pl.program_id(0) * part, part), part)
    for r in range(0, rows, tall):
        at = slice(r, r + tall)
        gossiped = hi[at, columns].astype(F32) + (lo[at, columns].astype(F32) - correction[at])
        velocity = 0.9 * m_ref[at, columns].astype(F32) + gossiped
        params_ref[at] = (g_ref[at, columns].astype(F32) - 0.7 * (gossiped + 0.9 * velocity)).astype(BF16)
        momentum_ref[at] = velocity.astype(BF16)


def outer_step(bas, fac, *whole):
    rows, cols = whole[0].shape
    part = min(512, cols)
    tile = pl.BlockSpec((rows, part), lambda i: (0, i))
    return pl.pallas_call(
        outer_kernel,
        grid=(cols // part,),
        out_shape=(jax.ShapeDtypeStruct((rows, cols), BF16),) * 2,
        in_specs=[
            pl.BlockSpec(bas.shape, lambda i: (0, 0)),
            pl.BlockSpec((fac.shape[0], part), lambda i: (0, i)),
        ]
        + [pl.BlockSpec(memory_space=pltpu.VMEM)] * len(whole),
        out_specs=(tile, tile),
        scratch_shapes=[pltpu.VMEM((rows, part), F32)],
        compiler_params=pltpu.CompilerParams(vmem_limit_bytes=12 << 20),
        cost_estimate=pl.CostEstimate(
            flops=2 * fac.shape[0] * rows * cols, bytes_accessed=4 * rows * cols, transcendentals=0
        ),
    )(bas, fac, *(pltpu.with_memory_space_constraint(x, pltpu.VMEM) for x in whole))


def on_device(global_params, local_params, momentum, init_factors, seeds, plan, round_index):
    shape = global_params.shape
    g, l, m = (x.reshape(shape[-2:]) for x in (global_params, local_params, momentum))
    turns = jnp.arange(plan.shape[0], dtype=jnp.int32)
    offset = jnp.sum(jnp.where(turns == lax.rem(round_index, plan.shape[0]), plan, 0))
    levels = lax.axis_size("island").bit_length() - 1
    shards = lax.axis_size("fsdp")
    which_bit = sum((offset > 1 << level).astype(jnp.int32) for level in range(levels))
    branches = [functools.partial(gossip, level, shards) for level in range(levels)]
    warm, fac, bas, *whole = lax.switch(which_bit, branches, seeds, g, l, m, init_factors[:, 0])
    params, velocity = outer_step(bas, fac, *whole)
    return params.reshape(shape), velocity.reshape(shape), warm[None, None]


def solution(mesh):
    return jax.shard_map(
        on_device,
        mesh=mesh,
        in_specs=(
            P("island", None, "fsdp", None),
            P("island", None, "fsdp", None),
            P("island", None, "fsdp", None),
            P(),
            P(),
            P(),
            P(),
        ),
        out_specs=(
            P("island", None, "fsdp", None),
            P("island", None, "fsdp", None),
            P("island", None, None, None),
        ),
        check_vma=False,
    )
```

```python
import functools

import jax
import jax.numpy as jnp
from jax import lax
from jax.experimental import pallas as pl
from jax.experimental.pallas import tpu as pltpu
from jax.sharding import PartitionSpec as P

ITERS = 3
MESH = pl.DeviceIdType.MESH
F32, BF16 = jnp.float32, jnp.bfloat16
NT = (((1,), (1,)), ((), ()))
NN = (((1,), (0,)), ((), ()))


def dot(a, b, dims):
    return lax.dot_general(a, b, dims, preferred_element_type=F32)


def rounded(x):
    return x.astype(BF16).astype(F32)


def three_parts(x):
    high = rounded(x)
    rest = x - high
    middle = rounded(rest)
    return jnp.concatenate([high, middle, rest - middle, jnp.zeros_like(x)], axis=0).astype(BF16)


def folded(x, rank):
    return x[0:rank] + x[rank : 2 * rank] + x[2 * rank : 3 * rank]


def cholesky(gram, rank):
    lower, inverse = {}, {}
    for j in range(rank):
        square = gram[j : j + 1, j : j + 1]
        for k in range(j):
            square = square - lower[j, k] * lower[j, k]
        inverse[j] = 1.0 / jnp.sqrt(square)
        for i in range(j + 1, rank):
            entry = gram[i : i + 1, j : j + 1]
            for k in range(j):
                entry = entry - lower[i, k] * lower[j, k]
            lower[i, j] = entry * inverse[j]
    return lower, inverse


def solved(factors, x):
    lower, inverse = factors
    rows = []
    for i in range(x.shape[0]):
        row = x[i : i + 1]
        for k in range(i):
            row = row - lower[i, k] * rows[k]
        rows.append(row * inverse[i])
    return jnp.concatenate(rows, axis=0)


def gossip_kernel(
    level, shards, seeds_ref, g_hbm, l_hbm, m_hbm, init_ref, warm_ref, fac_ref, bas_ref, hi, lo, g_ref, m_ref,
    l_buf, acc, p_out, p_in, rs_out, rs_in, gathered, grams,
    load_sem, m_sem, p_sem, rs_send, rs_recv, ag_send, ag_recv, gram_send, gram_recv,
):
    rank, cols = init_ref.shape[1:]
    rows = hi.shape[0]
    members = 2 * shards
    width = cols // members
    bundle = 4 if members % 4 == 0 else 1
    bundles = members // bundle
    island, shard = lax.axis_index("island"), lax.axis_index("fsdp")
    step = 1 << level
    side = lax.rem(lax.div(island, step), 2)
    me = side * shards + shard

    def device(k):
        return (island + (lax.div(k, shards) - side) * step, lax.rem(k, shards))

    def block(k):
        return pl.ds(pl.multiple_of(k * width, width), width)

    def columns(k):
        return pl.ds(pl.multiple_of(k * (bundle * width), bundle * width), bundle * width)

    mine = lax.div(me, bundle)

    def others(k, act):
        for j in range(bundle):
            b = k * bundle + j

            @pl.when(b != me)
            def _():
                act(b)

    def after(k):
        return lax.rem(me + k, members)

    barrier = pltpu.get_barrier_semaphore()

    @pl.loop(1, members)
    def _(k):
        pl.semaphore_signal(barrier, inc=1, device_id=device(after(k)), device_id_type=MESH)

    part = l_buf.shape[2]
    parts = cols // part
    tall = min(64, rows)

    def load(i, slot):
        at = pl.ds(pl.multiple_of(i * part, part), part)
        return (
            pltpu.make_async_copy(g_hbm.at[:, at], g_ref.at[:, at], load_sem.at[0, slot]),
            pltpu.make_async_copy(l_hbm.at[:, at], l_buf.at[slot], load_sem.at[1, slot]),
        )

    for copy in load(0, 0):
        copy.start()
    seed = seeds_ref[jnp.minimum(island, island + (1 - 2 * side) * step)]
    acc[...] = jnp.zeros_like(acc)

    def arrivals(ref, count, sem):
        pltpu.make_async_remote_copy(
            src_ref=ref.at[pl.ds(0, count)], dst_ref=ref.at[pl.ds(0, count)], send_sem=p_sem.at[0], recv_sem=sem,
            device_id=(island + (1 - 2 * side) * step, shard), device_id_type=MESH,
        ).wait_recv()

    def departures(ref, count, sem):
        pltpu.make_async_remote_copy(
            src_ref=ref.at[pl.ds(0, count)], dst_ref=ref.at[pl.ds(0, count)], send_sem=sem, recv_sem=p_sem.at[1],
            device_id=(island + (1 - 2 * side) * step, shard), device_id_type=MESH,
        ).wait_send()

    def right(at, factor):
        parts = three_parts(factor)
        return dot(hi[:, at], parts, NT) + dot(lo[:, at], parts, NT)

    @pl.loop(0, parts)
    def _(i):
        slot = lax.rem(i, 2)

        @pl.when(i + 1 < parts)
        def _():
            for copy in load(i + 1, 1 - slot):
                copy.start()

        for copy in load(i, slot):
            copy.wait()
        at = pl.ds(pl.multiple_of(i * part, part), part)
        factor = three_parts(init_ref[seed, :, at])
        for r in range(0, rows, tall):
            delta = g_ref[r : r + tall, at].astype(F32) - l_buf[slot, r : r + tall].astype(F32)
            high = delta.astype(BF16)
            low = (delta - high.astype(F32)).astype(BF16)
            hi[r : r + tall, at] = high
            lo[r : r + tall, at] = low
            acc[r : r + tall, 0 : 4 * rank] += dot(high, factor, NT) + dot(low, factor, NT)

    fill = pltpu.make_async_copy(m_hbm, m_ref, m_sem)
    fill.start()
    pl.semaphore_wait(barrier, members - 1)

    factors = None
    for turn in range(ITERS):
        product = folded(acc[...].T, rank)
        if turn:
            product = solved(factors, product)
        p_out[...] = product
        swap = pltpu.make_async_remote_copy(
            src_ref=p_out, dst_ref=p_in, send_sem=p_sem.at[0], recv_sem=p_sem.at[1],
            device_id=(island + (1 - 2 * side) * step, shard), device_id_type=MESH,
        )
        swap.start()
        swap.wait()
        left = product - p_in[...]

        left_parts = three_parts(left)

        def scatter(b):
            return pltpu.make_async_remote_copy(
                src_ref=rs_out.at[b], dst_ref=rs_in.at[me],
                send_sem=rs_send, recv_sem=rs_recv,
                device_id=device(b), device_id_type=MESH,
            )

        @pl.loop(1, bundles + 1)
        def _(s):
            k = lax.rem(mine + s, bundles)
            at = columns(k)
            raw = folded(dot(left_parts, hi[:, at], NN) + dot(left_parts, lo[:, at], NN), rank)
            for j in range(bundle):
                rs_out[pl.ds(k * bundle + j, 1)] = raw[None, :, j * width : (j + 1) * width]
            others(k, lambda b: scatter(b).start())

        rs_in[pl.ds(me, 1)] = rs_out[pl.ds(me, 1)]

        lane = lax.broadcasted_iota(jnp.int32, (rank, 128), 1)
        gram = jnp.zeros((rank, 128), F32)
        for j in range(rank):
            column = jnp.sum(left * left[j : j + 1], axis=1, keepdims=True)
            gram = jnp.where(lane == j, column, gram)
        grams[turn, pl.ds(shard, 1)] = gram[None]

        def gram_copy(k):
            to = lax.rem(shard + k, shards)
            return pltpu.make_async_remote_copy(
                src_ref=grams.at[turn, shard], dst_ref=grams.at[turn, shard],
                send_sem=gram_send, recv_sem=gram_recv.at[turn],
                device_id=(island, to), device_id_type=MESH,
            )

        @pl.loop(1, shards)
        def _(k):
            gram_copy(k).start()

        arrivals(rs_in, members - 1, rs_recv)
        gathered[pl.ds(me, 1)] = jnp.sum(rs_in[...], axis=0, keepdims=True)

        def gather(b):
            return pltpu.make_async_remote_copy(
                src_ref=gathered.at[me], dst_ref=gathered.at[me],
                send_sem=ag_send, recv_sem=ag_recv.at[mine],
                device_id=device(b), device_id_type=MESH,
            )

        def gathered_bundle(s):
            k = lax.rem(mine + bundles - s, bundles)

            @pl.when(s > 0)
            def _():
                arrivals(gathered, bundle, ag_recv.at[k])

            if bundle > 1:

                @pl.when(s == 0)
                def _():
                    arrivals(gathered, bundle - 1, ag_recv.at[k])

            return k

        @pl.loop(0, bundles)
        def _(s):
            others(lax.rem(mine + s, bundles), lambda b: gather(b).start())

        def normaliser():
            arrivals(grams.at[turn], shards - 1, gram_recv.at[turn])
            return cholesky(jnp.sum(grams[turn], axis=0), rank)

        factors = normaliser()
        if turn < ITERS - 1:

            @pl.loop(0, bundles)
            def _(s):
                k = gathered_bundle(s)
                factor = jnp.concatenate([gathered[k * bundle + j] for j in range(bundle)], axis=1)
                total = right(columns(k), factor)

                @pl.when(s == 0)
                def _():
                    acc[:, 0 : 4 * rank] = total

                @pl.when(s > 0)
                def _():
                    acc[:, 0 : 4 * rank] += total

        else:
            basis = 0.5 * solved(factors, left)
            high = rounded(basis)
            stack = jnp.concatenate([high, high, basis - high, jnp.zeros_like(basis)], axis=0)
            bas_ref[...] = jnp.concatenate([stack, jnp.zeros((128 - 4 * rank, rows), F32)], axis=0).T.astype(BF16)

            def finish(b):
                at = block(b)
                factor = solved(factors, gathered[b])
                warm_ref[:, at] = factor
                high = rounded(factor)
                fac_ref[:, at] = jnp.concatenate([high, factor - high, high, jnp.zeros_like(high)], axis=0).astype(BF16)

            @pl.loop(0, bundles)
            def _(s):
                k = gathered_bundle(s)
                for j in range(bundle):
                    finish(k * bundle + j)

        departures(rs_out, members - 1, rs_send)
        departures(gathered, members - 1, ag_send)
        departures(grams.at[turn], shards - 1, gram_send)

    fill.wait()


def gossip(level, shards, seeds, g, l, m, init):
    rows, cols = g.shape
    rank = init.shape[1]
    members = 2 * shards
    width = cols // members
    bundles = members // 4 if members % 4 == 0 else members
    part = min(1024, cols)
    vmem = pl.BlockSpec(memory_space=pltpu.VMEM)
    hbm = pl.BlockSpec(memory_space=pl.ANY)
    dma = pltpu.SemaphoreType.DMA
    return pl.pallas_call(
        functools.partial(gossip_kernel, level, shards),
        out_shape=(
            jax.ShapeDtypeStruct((rank, cols), F32),
            jax.ShapeDtypeStruct((4 * rank, cols), BF16),
            jax.ShapeDtypeStruct((rows, 128), BF16),
        )
        + (pltpu.VMEM((rows, cols), BF16),) * 4,
        in_specs=[pl.BlockSpec(memory_space=pltpu.SMEM), hbm, hbm, hbm, vmem],
        out_specs=(vmem,) * 7,
        scratch_shapes=[
            pltpu.VMEM((2, rows, part), BF16),
            pltpu.VMEM((rows, 128), F32),
            pltpu.VMEM((rank, rows), F32),
            pltpu.VMEM((rank, rows), F32),
            pltpu.VMEM((members, rank, width), F32),
            pltpu.VMEM((members, rank, width), F32),
            pltpu.VMEM((members, rank, width), F32),
            pltpu.VMEM((ITERS, shards, rank, 128), F32),
            dma((2, 2)),
            dma,
            dma((2,)),
            dma,
            dma,
            dma,
            dma((bundles,)),
            dma,
            dma((ITERS,)),
        ],
        compiler_params=pltpu.CompilerParams(
            collective_id=level + 1, has_side_effects=True, vmem_limit_bytes=12 << 20
        ),
        cost_estimate=pl.CostEstimate(
            flops=12 * ITERS * rank * rows * cols, bytes_accessed=4 * rows * cols, transcendentals=0
        ),
    )(seeds, g, l, m, init)


def outer_kernel(bas_ref, fac_ref, hi, lo, g_ref, m_ref, params_ref, momentum_ref):
    depth = fac_ref.shape[0]
    rows, part = params_ref.shape
    factor = fac_ref[...]
    tall = min(64, rows)
    columns = pl.ds(pl.multiple_of(pl.program_id(0) * part, part), part)
    for r in range(0, rows, tall):
        at = slice(r, r + tall)
        correction = dot(bas_ref[at, 0:depth], factor, NN)
        gossiped = hi[at, columns].astype(F32) + (lo[at, columns].astype(F32) - correction)
        velocity = 0.9 * m_ref[at, columns].astype(F32) + gossiped
        params_ref[at] = (g_ref[at, columns].astype(F32) - 0.7 * (gossiped + 0.9 * velocity)).astype(BF16)
        momentum_ref[at] = velocity.astype(BF16)


def outer_step(bas, fac, *whole):
    rows, cols = whole[0].shape
    part = min(512, cols)
    tile = pl.BlockSpec((rows, part), lambda i: (0, i))
    return pl.pallas_call(
        outer_kernel,
        grid=(cols // part,),
        out_shape=(jax.ShapeDtypeStruct((rows, cols), BF16),) * 2,
        in_specs=[
            pl.BlockSpec(bas.shape, lambda i: (0, 0)),
            pl.BlockSpec((fac.shape[0], part), lambda i: (0, i)),
        ]
        + [pl.BlockSpec(memory_space=pltpu.VMEM)] * len(whole),
        out_specs=(tile, tile),
        compiler_params=pltpu.CompilerParams(vmem_limit_bytes=12 << 20),
        cost_estimate=pl.CostEstimate(
            flops=2 * fac.shape[0] * rows * cols, bytes_accessed=4 * rows * cols, transcendentals=0
        ),
    )(bas, fac, *(pltpu.with_memory_space_constraint(x, pltpu.VMEM) for x in whole))


def on_device(global_params, local_params, momentum, init_factors, seeds, plan, round_index):
    shape = global_params.shape
    g, l, m = (x.reshape(shape[-2:]) for x in (global_params, local_params, momentum))
    turns = jnp.arange(plan.shape[0], dtype=jnp.int32)
    offset = jnp.sum(jnp.where(turns == lax.rem(round_index, plan.shape[0]), plan, 0))
    levels = lax.axis_size("island").bit_length() - 1
    shards = lax.axis_size("fsdp")
    which_bit = sum((offset > 1 << level).astype(jnp.int32) for level in range(levels))
    branches = [functools.partial(gossip, level, shards) for level in range(levels)]
    warm, fac, bas, *whole = lax.switch(which_bit, branches, seeds, g, l, m, init_factors[:, 0])
    params, velocity = outer_step(bas, fac, *whole)
    return params.reshape(shape), velocity.reshape(shape), warm[None, None]


def solution(mesh):
    return jax.shard_map(
        on_device,
        mesh=mesh,
        in_specs=(
            P("island", None, "fsdp", None),
            P("island", None, "fsdp", None),
            P("island", None, "fsdp", None),
            P(),
            P(),
            P(),
            P(),
        ),
        out_specs=(
            P("island", None, "fsdp", None),
            P("island", None, "fsdp", None),
            P("island", None, None, None),
        ),
        check_vma=False,
    )
```
